128 devices in a mesh: node: 16 (over x_hi, z, core), local: 8 (over y, x_lo).
Axes of the slice: x: 4 (x_hi: 2, x_lo: 2; x = x_hi * 2 + x_lo), y: 4, z: 4, core: 2. Of those that a mesh axis runs over, the one named last changes fastest.
Arguments:
- tokens: bfloat16 [16384, 8192], P(('node', 'local')), may hold values from -24 to 24
- upstream: bfloat16 [16384, 8192], P(('node', 'local')), may hold values from -1.5 to 1.5
- router_probs: float32 [16384, 64], P(('node', 'local')), may hold values from 0.01 to 0.3
- expert_ids: int32 [16384, 2], P(('node', 'local')), may hold values from 0 to 63, as said below
- slot_index: int32 [16384, 2], P(('node', 'local')), may hold values from -1 to 3, as said below
- w_in: bfloat16 [2, 8192, 16384], P(None, 'local', 'node'), may hold values from -0.0625 to 0.0625
- w_out: bfloat16 [2, 16384, 8192], P(None, 'node', 'local'), may hold values from -0.046875 to 0.046875
- router_weight: bfloat16 [8192, 64], replicated, may hold values from -0.125 to 0.125
Outputs:
- token_grads: bfloat16 [16384, 8192], P(('node', 'local'))
- w_in_grad: bfloat16 [2, 8192, 16384], P(None, 'local', 'node')
- w_out_grad: bfloat16 [2, 16384, 8192], P(None, 'node', 'local')
- router_grad: float32 [8192, 64], P(('node', 'local'))
The draws below stay inside these ranges and needn't reach their ends.
Inputs may be any that keep to these rules, and one draw needn't show every extreme that they name: `expert_ids`: each token names two different experts. `slot_index`: an assignment to an expert under 2 has as slot its rank among its device's 128 tokens' assignments to that expert, in an order drawn at random, and -1 when that rank is 4 or more; every assignment to another expert has -1. In every draw some expert under 2 fills all 4 slots from every device.
All inputs are finite; a program needn't handle non-finite values.
Results may differ from the reference program's by a relative error of at most 0.017.
Values may be sent and summed in bfloat16 or wider, within the bound.
No kernel may reach another device: no remote copies, remote signals or barrier semaphores. Data moves between devices by JAX's collectives and lax.ppermute only.
A program may use at most 128 MiB of HBM per device.

```python
import math
import jax
import jax.numpy as jnp
from jax import lax

D = 8192
FF = 16384
EXP_ALL = 64
FLIGHT = 2
TOK_DEV = 128
CAP = 4
TOKENS = 16384


def routing_tables(key):
    keys = jax.random.split(key, 6)
    blocks = TOKENS // TOK_DEV
    first_pick = jax.random.randint(keys[0], (TOKENS,), 0, EXP_ALL, dtype=jnp.int32)
    offset_one = jax.random.randint(keys[1], (TOKENS,), 1, EXP_ALL, dtype=jnp.int32)
    second_pick = (first_pick + offset_one) % EXP_ALL
    hot_expert = jax.random.randint(keys[2], (), 0, FLIGHT, dtype=jnp.int32)
    block_keys = jax.random.split(keys[3], blocks)
    order = jax.vmap(lambda subkey: jax.random.permutation(subkey, TOK_DEV).astype(jnp.int32))(block_keys).reshape(TOKENS)
    chosen = order < CAP
    offset_two = jax.random.randint(keys[4], (TOKENS,), 1, EXP_ALL, dtype=jnp.int32)
    first_pick = jnp.where(chosen, hot_expert, first_pick)
    clash = jnp.logical_and(chosen, second_pick == hot_expert)
    second_pick = jnp.where(clash, (hot_expert + offset_two) % EXP_ALL, second_pick)
    ids_table = jnp.stack([first_pick, second_pick], axis=1).astype(jnp.int32)
    rank_keys = jax.random.split(keys[5], blocks)
    priority = jax.vmap(lambda subkey: jax.random.permutation(subkey, 2 * TOK_DEV).astype(jnp.int32))(rank_keys)
    block_ids = ids_table.reshape(blocks, 2 * TOK_DEV)

    def ranking(ids_row, prio_row):
        same_expert = ids_row[:, None] == ids_row[None, :]
        ahead = prio_row[None, :] < prio_row[:, None]
        return jnp.sum(jnp.logical_and(same_expert, ahead).astype(jnp.int32), axis=1).astype(jnp.int32)
    ranks = jax.vmap(ranking)(block_ids, priority).reshape(TOKENS, 2)
    held = jnp.logical_and(ranks < CAP, ids_table < FLIGHT)
    slot_table = jnp.where(held, ranks, -1).astype(jnp.int32)
    return (ids_table, slot_table)


def draw_expert_ids(key, part):
    return routing_tables(key)[0]


def draw_slot_index(key, part):
    return routing_tables(key)[1]


def spiked(entries, stream_key, source, target, shards_of, factor):
    def block_of(dim):
        return (jnp.arange(entries.shape[dim]) // (entries.shape[dim] // shards_of)).reshape((-1,) + (1,) * (entries.ndim - 1 - dim))

    near = jax.random.permutation(stream_key, shards_of)[block_of(target)]
    far = (block_of(target) + shards_of // 2) % shards_of
    return jnp.where((block_of(source) == near) | (block_of(source) == far), factor * entries, entries)


def block_scale(stream_key, dims, pieces, least, high):
    def one(axis_at, parts):
        steps = jax.random.uniform(jax.random.fold_in(jax.random.fold_in(stream_key, 6), axis_at), (parts,), jnp.float32, least / len(pieces), high / len(pieces))
        return jnp.repeat(jnp.exp(steps), dims[axis_at] // parts).reshape((-1,) + (1,) * (len(dims) - axis_at - 1))

    gain = one(*pieces[0])
    for cut in pieces[1:]:
        gain = gain * one(*cut)
    return gain


def scatter_about(own_key, shape, scale, bound, cuts=(), held_as=jnp.bfloat16):
    array = jax.random.normal(own_key, shape, jnp.float32) * scale
    if len(cuts) > 0:
        array = block_scale(own_key, shape, cuts, -0.22, 0.18) * array
    return jnp.clip(array, min=-bound, max=bound).astype(held_as)


def bell_draw_with(stream_key, extent, spread, limit, cuts, heavy, kind=jnp.bfloat16):
    result = spread * jax.random.normal(stream_key, extent, jnp.float32)
    if cuts:
        result = result * block_scale(stream_key, extent, cuts, -0.22, 0.18)
    return jnp.clip(spiked(result, jax.random.fold_in(stream_key, 3), *heavy), -limit, limit).astype(kind)


def setup_inputs(seed: int = 0) -> dict:
    arg_keys = jax.random.split(jax.random.key(seed), 9)
    tokens = bell_draw_with(arg_keys[0], (TOKENS, D), 1.0, 24.0, ((0, 128),), (0, 1, 128, 5.5))
    upstream = scatter_about(arg_keys[1], (TOKENS, D), 0.25, 1.5, ((0, 128),))
    router_probs = jnp.clip(jnp.exp(math.log(0.3) - 3.4011974 * jax.random.uniform(arg_keys[2], (TOKENS, EXP_ALL), jnp.float32) ** block_scale(arg_keys[2], (TOKENS, EXP_ALL), ((0, 128),), -0.2, 0.2)), 0.01, 0.3)
    expert_ids = draw_expert_ids(jax.random.fold_in(arg_keys[8], 71), 0)
    slot_index = draw_slot_index(jax.random.fold_in(arg_keys[8], 71), 0)
    w_in = scatter_about(arg_keys[5], (FLIGHT, D, FF), D ** -0.5, 0.0625, ((1, 8), (2, 16)))
    w_out = scatter_about(arg_keys[6], (FLIGHT, FF, D), FF ** -0.5, 0.046875, ((1, 16), (2, 8)))
    router_weight = scatter_about(arg_keys[7], (D, EXP_ALL), (D // 4) ** -0.5, 0.125)
    return {"tokens": tokens, "upstream": upstream, "router_probs": router_probs, "expert_ids": expert_ids, "slot_index": slot_index, "w_in": w_in, "w_out": w_out, "router_weight": router_weight}


root_two_pi = math.sqrt(2.0 / math.pi)
cubic_coef = 0.044715

def gelu_pair(pre):
    inner = root_two_pi * (pre + cubic_coef * pre * pre * pre)
    tangent = jnp.tanh(inner)
    value = 0.5 * pre * (1.0 + tangent)
    slope = 0.5 * (1.0 + tangent) + 0.5 * pre * (1.0 - tangent * tangent) * root_two_pi * (1.0 + 3.0 * cubic_coef * pre * pre)
    return (value, slope)

def reference(tokens, upstream, router_probs, expert_ids, slot_index, w_in, w_out, router_weight):
    span = TOKENS // TOK_DEV * CAP
    owner = (jnp.arange(TOKENS, dtype=jnp.int32) // TOK_DEV).astype(jnp.int32)[:, None]
    is_kept = slot_index >= 0
    safe_expert = jnp.where(is_kept, expert_ids, 0).astype(jnp.int32)
    position = (owner * CAP + jnp.where(is_kept, slot_index, 0)).astype(jnp.int32)
    flat_place = jnp.where(is_kept, safe_expert * span + position, FLIGHT * span).astype(jnp.int32)
    token_numbers = jnp.broadcast_to(jnp.arange(TOKENS, dtype=jnp.int32)[:, None], (TOKENS, 2))
    token_of = jnp.full((FLIGHT * span,), -1, jnp.int32).at[flat_place.reshape(-1)].set(token_numbers.reshape(-1), mode='drop').reshape(FLIGHT, span)

    def expert(packed):
        expert_number, first_matrix, second_matrix, row_tokens = packed
        valid = row_tokens >= 0
        safe_rows = jnp.where(valid, row_tokens, 0).astype(jnp.int32)
        rows_in = jnp.where(valid[:, None], tokens[safe_rows], jnp.zeros((), tokens.dtype))
        rows_up = jnp.where(valid[:, None], upstream[safe_rows], jnp.zeros((), upstream.dtype))
        gate_rows = jnp.where(valid, router_probs[safe_rows, expert_number], jnp.zeros((), jnp.float32)).astype(jnp.bfloat16)
        gate_wide = gate_rows.astype(jnp.float32)[:, None]
        pre = jnp.dot(rows_in, first_matrix, preferred_element_type=jnp.float32)
        value, slope = gelu_pair(pre)
        act = value.astype(jnp.bfloat16)
        upw = jnp.dot(rows_up, second_matrix.T, preferred_element_type=jnp.float32)
        scores = lax.optimization_barrier(jnp.sum(act.astype(jnp.float32) * upw, axis=1))
        pre_grad = (gate_wide * upw * slope).astype(jnp.bfloat16)
        out_grad = (gate_wide * rows_up.astype(jnp.float32)).astype(jnp.bfloat16)
        second_grad = jnp.dot(act.T, out_grad, preferred_element_type=jnp.float32).astype(jnp.bfloat16)
        first_grad = jnp.dot(rows_in.T, pre_grad, preferred_element_type=jnp.float32).astype(jnp.bfloat16)
        row_grads = jnp.dot(pre_grad, first_matrix.T, preferred_element_type=jnp.float32).astype(jnp.bfloat16)
        return (first_grad, second_grad, row_grads, scores)
    w_in_grad, w_out_grad, row_grads, scores = lax.map(expert, (jnp.arange(FLIGHT, dtype=jnp.int32), w_in, w_out, token_of))
    combined = jnp.zeros((TOKENS, D), jnp.float32)
    for which in range(2):
        picked = row_grads[safe_expert[:, which], position[:, which]].astype(jnp.float32)
        combined = combined + jnp.where(is_kept[:, which, None], picked, jnp.zeros((), jnp.float32))
    gate_grad = jnp.where(is_kept, scores[safe_expert, position], jnp.zeros((), jnp.float32))
    expert_iota = jnp.arange(EXP_ALL, dtype=jnp.int32)
    matches = expert_ids[:, :, None] == expert_iota[None, None, :]
    prob_grad = lax.optimization_barrier(jnp.sum(jnp.where(matches, gate_grad[:, :, None], jnp.zeros((), jnp.float32)), axis=1))
    centred = prob_grad - lax.optimization_barrier(jnp.sum(router_probs * prob_grad, axis=1, keepdims=True))
    logit_grad = (router_probs * centred).astype(jnp.bfloat16)
    router_grad = jnp.dot(tokens.T, logit_grad, preferred_element_type=jnp.float32)
    router_part = jnp.dot(logit_grad, router_weight.T, preferred_element_type=jnp.float32)
    token_grads = (combined + router_part).astype(jnp.bfloat16)
    return (token_grads, w_in_grad, w_out_grad, router_grad)
```

```python
import math

import jax
import jax.numpy as jnp
from jax import lax
from jax.sharding import PartitionSpec as P

CAP = 4


root_two_pi = math.sqrt(2.0 / math.pi)
cubic_coef = 0.044715
bf16 = jnp.bfloat16
f32 = jnp.float32


def gelu_pair(pre):
    inner = root_two_pi * (pre + cubic_coef * pre * pre * pre)
    tangent = jnp.tanh(inner)
    value = 0.5 * pre * (1.0 + tangent)
    slope = 0.5 * (1.0 + tangent) + 0.5 * pre * (1.0 - tangent * tangent) * root_two_pi * (
        1.0 + 3.0 * cubic_coef * pre * pre
    )
    return (value, slope)


def contract(left, right, left_dim, right_dim):
    return lax.dot_general(
        left, right, (((left_dim,), (right_dim,)), ((), ())), preferred_element_type=f32
    )


def node_of(x_hi, z, core):
    return (x_hi * 4 + z % 4) * 2 + core


def send_core(value):
    return lax.ppermute(value, "node", [(i, i ^ 1) for i in range(16)])


def send_x_hi(value):
    return lax.ppermute(value, "node", [(i, i ^ 8) for i in range(16)])


def send_z(value, step):
    return lax.ppermute(
        value, "node", [(i, node_of(i // 8, i // 2 + step, i % 2)) for i in range(16)]
    )


def send_x_lo(value):
    return lax.ppermute(value, "local", [(i, i ^ 1) for i in range(8)])


def send_y(value, step):
    return lax.ppermute(value, "local", [(i, (i // 2 + step) % 4 * 2 + i % 2) for i in range(8)])


def gather_node(value):
    pair = jnp.stack([value, send_x_hi(value)])
    ring = jnp.stack([pair, send_z(pair, 3), send_z(pair, 2), send_z(pair, 1)])
    return jnp.stack([ring, send_core(ring)])


def scatter_sum_node(terms):
    sent = terms.astype(bf16)
    half = terms[0] + send_core(sent[1]).astype(f32)
    sent = half.astype(bf16)
    ring = half[0]
    for step in range(1, 4):
        ring = ring + send_z(sent[step], step).astype(f32)
    return ring[0] + send_x_hi(ring[1].astype(bf16)).astype(f32)


def pick(value, index, axis):
    return lax.dynamic_index_in_dim(value, index, axis, keepdims=False)


def scatter_sum_y(parts, y):
    total = pick(parts, y, 1).astype(f32)
    for step in range(1, 4):
        total = total + send_y(pick(parts, (y + step) % 4, 1), step).astype(f32)
    return total


def gather_y(value, y):
    out = jnp.broadcast_to(value[:, None], (2, 4) + value.shape[1:])
    for step in range(1, 4):
        out = lax.dynamic_update_index_in_dim(out, send_y(value, step), (y - step) % 4, 1)
    return out


def scatter_sum_x(parts, x, axis):
    mine = pick(parts, x, axis).astype(f32)
    return mine + send_x_lo(pick(parts, 1 - x, axis).astype(bf16)).astype(f32)


def gather_x(value, x, axis):
    other = send_x_lo(value)
    return jnp.stack(
        [jnp.where(x == 0, value, other), jnp.where(x == 0, other, value)], axis=axis
    )


def local(tokens, upstream, router_probs, expert_ids, slot_index, w_in, w_out, router_weight):
    token_count, model_width = tokens.shape
    flight = w_in.shape[0]
    feature_width = w_in.shape[1]
    capacity = CAP
    node = lax.axis_index("node")
    spot = lax.axis_index("local")
    y, x = spot // 2, spot % 2
    span = 8 * capacity

    is_kept = slot_index >= 0
    target = jnp.where(is_kept, expert_ids * capacity + slot_index, -1)
    slot_iota = jnp.arange(flight * capacity, dtype=jnp.int32)
    slot_hits = slot_iota[:, None, None] == target[None, :, :]
    placing = jnp.any(slot_hits, axis=2).astype(bf16)
    send_in = jnp.dot(placing, tokens, preferred_element_type=f32).astype(bf16)
    send_up = jnp.dot(placing, upstream, preferred_element_type=f32).astype(bf16)
    expert_count = router_probs.shape[1]
    expert_iota = jnp.arange(expert_count, dtype=jnp.int32)
    matches = expert_ids[:, :, None] == expert_iota[None, None, :]
    slot_probs = jnp.sum(
        jnp.where(
            jnp.any(slot_hits, axis=2),
            jnp.repeat(router_probs[:, :flight].T, capacity, axis=0),
            jnp.zeros((), f32),
        ),
        axis=1,
    ).astype(bf16)
    send_gate = jnp.broadcast_to(slot_probs[None, :, None], (8, 8, feature_width))
    blocks = jnp.stack([send_in, send_up]).reshape(16, 8, feature_width).transpose(1, 0, 2)
    got = lax.all_to_all(
        jnp.concatenate([blocks, send_gate], axis=1), "local", 0, 0, tiled=True
    )
    got = (
        got.reshape(8, 3, flight, capacity, feature_width)
        .transpose(1, 2, 0, 3, 4)
        .reshape(3, flight, span, feature_width)
    )
    gates = gather_node(got[2, :, :, :128])
    rows_in, rows_up, gate_wide, pre_grads, acts, back, scores = [], [], [], [], [], [], []
    parts = []
    for e in range(flight):
        rows = gather_node(got[:2, e])
        rows_in.append(rows[..., 0, :, :].reshape(-1, feature_width))
        rows_up.append(rows[..., 1, :, :].reshape(-1, feature_width))
        gate_wide.append(gates[..., e, :, :].reshape(-1, 128))
        pre_part = contract(rows_in[e], w_in[e], 1, 0).astype(bf16)
        upw_part = contract(rows_up[e], w_out[e], 1, 1).astype(bf16)
        parts.append(jnp.stack([pre_part, upw_part]).reshape(2, 4, 2, 64, -1))

    sums = [
        scatter_sum_x(scatter_sum_y(parts[0], y), x, 1),
        scatter_sum_y(scatter_sum_x(parts[1], x, 2).astype(bf16), y),
    ]
    blocks = []
    for e in range(flight):
        pre, upw = sums[e][0], sums[e][1]
        gate = lax.dynamic_slice_in_dim(gate_wide[e], spot * 64, 64, 0)[:, :1].astype(f32)
        value, slope = gelu_pair(pre)
        act = value.astype(bf16)
        pre_grad = (gate * upw * slope).astype(bf16)
        scores.append(jnp.sum(act.astype(f32) * upw, axis=1))
        blocks.append(jnp.stack([act, pre_grad]))
    wide = [
        gather_y(gather_x(blocks[0], x, 1), y),
        gather_x(gather_y(blocks[1], y), x, 2),
    ]
    rel = jnp.arange(16, dtype=jnp.int32)
    rel_core, rel_z, rel_x = rel // 8, rel // 2 % 4, rel % 2
    node_core, node_z, node_x = node % 2, node // 2 % 4, node // 8
    abs_of_rel = ((node_x ^ rel_x) * 4 + (node_z + rel_z) % 4) * 2 + (node_core ^ rel_core)
    to_abs = rel[:, None] == abs_of_rel[None, :]
    mine = lax.dynamic_slice_in_dim(to_abs, spot * 2, 2, 1)
    score = jnp.stack(scores).reshape(flight, 2, 8, capacity).transpose(1, 2, 0, 3)
    score = jnp.sum(
        jnp.where(mine[:, :, None, None, None], score[None], jnp.zeros((), f32)), axis=1
    ).reshape(128, flight * capacity)
    own_scores = jnp.sum(
        lax.all_to_all(score, ("node", "local"), 0, 0, tiled=True), axis=0
    )

    gate_grad = jnp.sum(
        jnp.where(slot_hits, own_scores[:, None, None], jnp.zeros((), f32)), axis=0
    )
    prob_grad = jnp.sum(
        jnp.where(matches, gate_grad[:, :, None], jnp.zeros((), f32)), axis=1
    )
    centred = prob_grad - jnp.sum(router_probs * prob_grad, axis=1, keepdims=True)
    logit_grad = (router_probs * centred).astype(bf16)
    first = jnp.where(is_kept[:, :1], jnp.arange(2) == 0, jnp.arange(2) == 1)
    once = jnp.any(slot_hits & first[None], axis=2).astype(bf16)
    logit_rows = jnp.dot(once, logit_grad, preferred_element_type=f32).astype(bf16)
    all_logits = lax.all_to_all(
        jnp.broadcast_to(logit_rows[None], (128,) + logit_rows.shape),
        ("node", "local"),
        0,
        0,
        tiled=True,
    )
    all_logits = contract(
        to_abs.astype(bf16), all_logits.reshape(16, -1), 0, 0
    ).astype(bf16).reshape(16, 8, flight, capacity, expert_count)
    router_terms = jnp.zeros((), f32)
    for e in range(flight):
        columns = lax.dynamic_slice_in_dim(rows_in[e], node * 64, 64, 1)
        router_terms = router_terms + contract(
            columns, all_logits[:, :, e].reshape(-1, expert_count), 0, 0
        )
    router_grad = lax.ppermute(
        router_terms, ("node", "local"), [(i, i % 8 * 16 + i // 8) for i in range(128)]
    )

    for e in range(flight):
        act, pre_grad = wide[e].reshape(2, -1, wide[e].shape[-1])
        acts.append(act)
        pre_grads.append(pre_grad)
        row_terms = contract(pre_grad, w_in[e], 1, 1)
        back.append(scatter_sum_node(row_terms.reshape(2, 4, 2, span, feature_width)))
    out_grad = [
        (rows_up[e].astype(f32) * gate_wide[e][:, :1].astype(f32)).astype(bf16)
        for e in range(flight)
    ]
    w_out_grad = jnp.einsum(
        "erf,erd->efd", jnp.stack(acts), jnp.stack(out_grad), preferred_element_type=f32
    ).astype(bf16)
    w_in_grad = jnp.einsum(
        "erd,erf->edf", jnp.stack(rows_in), jnp.stack(pre_grads), preferred_element_type=f32
    ).astype(bf16)

    row_grads = jnp.stack(back).astype(bf16).reshape(flight, 8, capacity, feature_width)
    home = lax.all_to_all(
        row_grads.transpose(1, 0, 2, 3).reshape(8, flight * capacity, feature_width),
        "local",
        0,
        0,
        tiled=True,
    )
    home = home.transpose(1, 0, 2).reshape(flight * capacity, model_width)
    combined = contract(placing, home, 0, 0)
    router_part = contract(logit_grad, router_weight, 1, 1)
    token_grads = (combined + router_part).astype(bf16)
    return (token_grads, w_in_grad, w_out_grad, router_grad)


def solution(mesh):
    in_specs = (
        P(("node", "local"), None),
        P(("node", "local"), None),
        P(("node", "local"), None),
        P(("node", "local"), None),
        P(("node", "local"), None),
        P(None, "local", "node"),
        P(None, "node", "local"),
        P(),
    )
    out_specs = (
        P(("node", "local"), None),
        P(None, "local", "node"),
        P(None, "node", "local"),
        P(("node", "local"), None),
    )
    return jax.shard_map(local, mesh=mesh, in_specs=in_specs, out_specs=out_specs, check_vma=False)
```

```python
import math

import jax
import jax.numpy as jnp
from jax import lax
from jax.experimental import pallas as pl
from jax.experimental.pallas import tpu as pltpu
from jax.sharding import PartitionSpec as P

CAP = 4


root_two_pi = math.sqrt(2.0 / math.pi)
cubic_coef = 0.044715
bf16 = jnp.bfloat16
f32 = jnp.float32


def gelu_pair(pre):
    inner = root_two_pi * (pre + cubic_coef * pre * pre * pre)
    tangent = jnp.tanh(inner)
    value = 0.5 * pre * (1.0 + tangent)
    slope = 0.5 * (1.0 + tangent) + 0.5 * pre * (1.0 - tangent * tangent) * root_two_pi * (
        1.0 + 3.0 * cubic_coef * pre * pre
    )
    return (value, slope)


def contract(left, right, left_dim, right_dim):
    return lax.dot_general(
        left, right, (((left_dim,), (right_dim,)), ((), ())), preferred_element_type=f32
    )


same_core = [[place * 2 + core for place in range(8)] for core in range(2)]


def send_core(value):
    return lax.ppermute(value, "node", [(i, i ^ 1) for i in range(16)])


def send_x_hi(value):
    return lax.ppermute(value, "node", [(i, i ^ 8) for i in range(16)])


def send_x(value):
    return lax.ppermute(value, "local", [(i, i ^ 1) for i in range(8)])


def trade_places(blocks):
    return lax.all_to_all(blocks, "node", 0, 0, tiled=True, axis_index_groups=same_core)


def send_z(value, step):
    pairs = [(i, (i // 8 * 4 + (i // 2 + step) % 4) * 2 + i % 2) for i in range(16)]
    return lax.ppermute(value, "node", pairs)


def send_y(value, step):
    return lax.ppermute(value, "local", [(i, (i // 2 + step) % 4 * 2 + i % 2) for i in range(8)])


def ring(value, send):
    return [value] + [send(value, 4 - step) for step in range(1, 4)]


def turn(start):
    places = jnp.arange(4)
    return (places[:, None] + start) % 4 == places[None, :]


def turned(value, hit, axis):
    value = jnp.moveaxis(value, axis, 0)
    hit = hit.reshape((4, 4) + (1,) * (value.ndim - 1))
    return jnp.moveaxis(jnp.sum(jnp.where(hit, value[None], jnp.zeros((), f32)), axis=1), 0, axis)


def trade_all(value):
    return lax.all_to_all(value, ("node", "local"), 0, 0, tiled=True)


def spread(value, count):
    return jnp.broadcast_to(value[None], (count,) + value.shape)


def after(value, *others):
    return lax.optimization_barrier((value,) + others)[0]


def together(*values):
    return lax.optimization_barrier(values)


def up(value):
    return value.astype(f32)


def pick(value, index, axis):
    return lax.dynamic_index_in_dim(value, index, axis, keepdims=False)


def join_x(mine, other, x, axis):
    return jnp.stack([jnp.where(x == 0, mine, other), jnp.where(x == 0, other, mine)], axis=axis)


def matmul(left, right, left_dim=1, right_dim=0):
    return contract(left, right, left_dim, right_dim)


tile = 256
room = 58 * 1024 * 1024


def call(kernel, grid, in_specs, out_specs, out_shape, flops, scratch=(), aliases=None):
    return pl.pallas_call(
        kernel,
        grid=grid,
        in_specs=in_specs,
        out_specs=out_specs,
        out_shape=out_shape,
        scratch_shapes=list(scratch),
        input_output_aliases=aliases or {},
        compiler_params=pltpu.CompilerParams(vmem_limit_bytes=room),
        cost_estimate=pl.CostEstimate(flops=flops, bytes_accessed=flops // 256, transcendentals=0),
    )


def row_specs():
    return [pl.BlockSpec((8, 32, 1024), lambda j, k=k: (0, k, 0)) for k in (0, 1, 0, 1)]


scalar_spec = pl.BlockSpec(memory_space=pltpu.SMEM)


step_width = 256


def weight_specs(e):
    return [
        pl.BlockSpec((1, 1024, step_width), lambda j: (e, 0, j)),
        pl.BlockSpec((1, step_width, 1024), lambda j: (e, j, 0)),
    ]


def projections(refs, rows):
    into, out_of = refs[4:]

    @pl.when(pl.program_id(0) == 0)
    def _():
        for part in range(4):
            half = part // 2 * 256
            rows[part % 2, half : half + 256, :] = refs[part][...].reshape(256, 1024)

    return matmul(rows[0], into[0]), matmul(rows[1], out_of[0], 1, 1)


def project_whole(near, far, w_in, w_out, e, spots):
    def kernel(at, *refs):
        outs, rows, parts = refs[6:10], refs[10], refs[11]
        for which, part in enumerate(projections(refs[:6], rows)):
            parts[:, which] = part.astype(bf16).reshape(4, 128, step_width)
        for step in range(4):
            outs[step][...] = parts[lax.rem(at[0] + step, 4)]

    return call(
        kernel,
        (1024 // step_width,),
        [scalar_spec] + row_specs() + weight_specs(e),
        [pl.BlockSpec((2, 128, step_width), lambda j: (0, 0, j))] * 4,
        [jax.ShapeDtypeStruct((2, 128, 1024), bf16)] * 4,
        2 * 2 * 512 * 1024 * 1024,
        [pltpu.VMEM((2, 512, 1024), bf16), pltpu.VMEM((4, 2, 128, step_width), bf16)],
    )(spots, near, near, far, far, w_in, w_out)


def project_split(near, far, w_in, w_out, e, spots):
    def kernel(at, *refs):
        kept, sent, rows = refs[6:]
        first = at[1] == 0
        for which, part in enumerate(projections(refs[:6], rows)):
            part = part.astype(bf16).reshape(4, 2, 64, step_width)
            low, high = part[:, 0], part[:, 1]
            mine, other = jnp.where(first, low, high), jnp.where(first, high, low)
            for y in range(4):
                place = lax.rem(y + 4 - at[0], 4)
                kept[place, which] = mine[y]
                sent[place, which] = other[y]

    return call(
        kernel,
        (1024 // step_width,),
        [scalar_spec] + row_specs() + weight_specs(e),
        [pl.BlockSpec((4, 2, 64, step_width), lambda j: (0, 0, 0, j))] * 2,
        [jax.ShapeDtypeStruct((4, 2, 64, 1024), bf16)] * 2,
        2 * 2 * 512 * 1024 * 1024,
        [pltpu.VMEM((2, 512, 1024), bf16)],
    )(spots, near, near, far, far, w_in, w_out)


def wide_specs(pieces, which):
    if len(pieces) == 4:
        return [pl.BlockSpec((1, 128, 1024), lambda j: (which, 0, 0))] * 4
    return [pl.BlockSpec((4, 1, 64, 1024), lambda j: (0, which, 0, 0))] * 2


def lay_rows(pieces, at, rows):
    for step in range(4):
        base = lax.rem(at[0] + step, 4) * 128
        if len(pieces) == 4:
            rows[pl.ds(pl.multiple_of(base, 128), 128), :] = pieces[step][0]
        else:
            for x, piece in ((at[1], pieces[0]), (1 - at[1], pieces[1])):
                rows[pl.ds(pl.multiple_of(base + x * 64, 64), 64), :] = piece[step, 0]


def row_terms_of(pieces, w_in, e, spots):
    count = len(pieces)
    wide = 512

    def kernel(at, *refs):
        grads, into, kept, sent, rows = refs[:count], *refs[count:]

        @pl.when(pl.program_id(0) == 0)
        def _():
            lay_rows(grads, at, rows)

        terms = matmul(rows[...], into[0], 1, 1)
        for step in range(4):
            z = lax.rem(at[2] + step, 4)
            for x_hi in range(2):
                block = (step * 2 + x_hi if e == 0 else x_hi * 4 + step) * 32
                kept[x_hi, z] = terms[block : block + 32]
                sent[x_hi, z] = terms[256 + block : 288 + block].astype(bf16)

    shape = (2, 4, 32, 1024)
    return call(
        kernel,
        (1024 // wide,),
        [scalar_spec]
        + wide_specs(pieces, 1)
        + [pl.BlockSpec((1, wide, 1024), lambda j: (e, j, 0))],
        [pl.BlockSpec((2, 4, 32, wide), lambda j: (0, 0, 0, j))] * 2,
        [jax.ShapeDtypeStruct(shape, f32), jax.ShapeDtypeStruct(shape, bf16)],
        2 * 512 * 1024 * 1024,
        [pltpu.VMEM((512, 1024), bf16)],
    )(spots, *pieces, w_in)


def weight_grads(near, far, gates, pieces, e, spots, earlier=()):
    count = len(pieces)

    def kernel(at, in0, up0, in1, up1, gate, *refs):
        acts, grads, refs = refs[:count], refs[count : 2 * count], refs[2 * count + len(earlier) :]
        into, out_of, act_rows, grad_rows, out_rows = refs
        j = pl.program_id(0)

        @pl.when(j == 0)
        def _():
            lay_rows(acts, at, act_rows)
            lay_rows(grads, at, grad_rows)
            for half, ups in enumerate((up0, up1)):
                part = slice(256 * half, 256 * half + 256)
                out_rows[part, :] = (
                    up(ups[...].reshape(256, 1024)) * gate[part, :]
                ).astype(bf16)

        columns = pl.ds(pl.multiple_of(j * tile, tile), tile)
        into[0] = (
            matmul(in0[:, :, columns].reshape(256, tile), grad_rows[:256, :], 0, 0)
            + matmul(in1[:, :, columns].reshape(256, tile), grad_rows[256:, :], 0, 0)
        ).astype(bf16)
        out_of[0] = matmul(act_rows[:, columns], out_rows[...], 0, 0).astype(bf16)

    return call(
        kernel,
        (1024 // tile,),
        [scalar_spec]
        + row_specs()
        + [pl.BlockSpec((512, 1), lambda j: (0, 0))]
        + wide_specs(pieces, 0)
        + wide_specs(pieces, 1)
        + [pl.BlockSpec(memory_space=pl.ANY)] * len(earlier),
        [pl.BlockSpec((1, tile, 1024), lambda j: (e, j, 0))] * 2,
        [jax.ShapeDtypeStruct((2, 1024, 1024), bf16)] * 2,
        2 * 2 * 512 * 1024 * 1024,
        [pltpu.VMEM((512, 1024), bf16)] * 3,
        {6 + 2 * count + i: i for i in range(len(earlier))},
    )(spots, near, near, far, far, gates, *pieces, *pieces, *earlier)


def local(tokens, upstream, router_probs, expert_ids, slot_index, w_in, w_out, router_weight):
    token_count, model_width = tokens.shape
    flight = w_in.shape[0]
    feature_width = w_in.shape[1]
    capacity = CAP
    expert_count = router_probs.shape[1]
    node = lax.axis_index("node")
    spot = lax.axis_index("local")
    x_hi, z, core, y, x = node // 8, node // 2 % 4, node % 2, spot // 2, spot % 2
    spots = jnp.stack([y, x, z]).astype(jnp.int32)
    span = 8 * capacity

    is_kept = slot_index >= 0
    target = jnp.where(is_kept, expert_ids * capacity + slot_index, -1)
    slot_iota = jnp.arange(flight * capacity, dtype=jnp.int32)
    slot_hits = slot_iota[:, None, None] == target[None, :, :]
    placing = jnp.any(slot_hits, axis=2).astype(bf16)
    send_in = jnp.dot(placing, tokens, preferred_element_type=f32).astype(bf16)
    send_up = jnp.dot(placing, upstream, preferred_element_type=f32).astype(bf16)
    slot_probs = jnp.dot(placing, router_probs.astype(bf16), preferred_element_type=f32)
    same = contract(placing, placing, 1, 1)
    twins = same[:, 4:]
    counted = 1 - jnp.where(slot_iota < 4, 0, jnp.sum(same[:, :4], axis=1))[:, None]
    facts = jnp.pad(
        jnp.concatenate([slot_probs, twins, counted], axis=1).astype(bf16), ((0, 8), (0, 59))
    )
    blocks = jnp.stack([send_in, send_up]).reshape(16, 8, feature_width).transpose(1, 0, 2)
    got = lax.all_to_all(
        jnp.concatenate([blocks, spread(facts, 8)], axis=2), "local", 0, 0, tiled=True
    )
    facts = (
        got[:, :8, feature_width:].reshape(8, flight, capacity, 128)
        .transpose(1, 0, 2, 3)
        .reshape(8, 8, 128)
        .transpose(1, 0, 2)
        .reshape(8, feature_width)
    )
    got = (
        got[:, :, :feature_width]
        .reshape(8, 2, flight, capacity, feature_width)
        .transpose(2, 1, 0, 3, 4)
        .reshape(4 * span, feature_width)
    )
    packets = [got[: 2 * span], jnp.concatenate([got[2 * span :], facts])]

    pair0 = join_x(packets[0], send_x_hi(packets[0]), x_hi, 0)
    ring1 = jnp.stack(ring(packets[1], send_z))
    pair0, ring1 = together(pair0, ring1)
    near1 = join_x(ring1, send_x_hi(ring1), x_hi, 0).reshape(8, -1, feature_width)
    near0 = jnp.stack(ring(pair0, send_z)).reshape(8, -1, feature_width)
    near0, near1, turns = together(near0, near1, turn(z))
    near, far = [near0, near1], [send_core(near0), send_core(near1)]
    facts = (
        jnp.stack([near1[:, 2 * span :], far[1][:, 2 * span :]])
        .reshape(16, 8, 8, 128)
        .transpose(0, 2, 1, 3)
        .reshape(16, flight, span, 128)
    )
    facts = [
        facts[:, 0].reshape(2, 2, 4, span, 128).transpose(0, 2, 1, 3, 4).reshape(-1, 128),
        facts[:, 1].reshape(-1, 128),
    ]
    gates = [up(facts[e][:, e : e + 1]) for e in range(flight)]

    kept1, sent1 = project_split(near[1], far[1], w_in, w_out, 1, spots)
    other1 = send_x(sent1)
    parts0 = project_whole(after(near[0], sent1), far[0], w_in, w_out, 0, spots)
    got0 = [send_y(parts0[step], step) for step in range(1, 4)]
    other1, got0 = together(other1, got0)
    half0 = (up(parts0[0]) + sum(up(part) for part in got0)).reshape(2, 2, 64, -1)
    half1 = [up(kept1[step]) + up(other1[step]) for step in range(4)]
    sent0, sent1 = together(
        pick(half0, 1 - x, 1).astype(bf16), [half1[step].astype(bf16) for step in range(1, 4)]
    )
    other0, got1 = together(
        send_x(sent0), [send_y(part, step + 1) for step, part in enumerate(sent1)]
    )
    sum0 = pick(half0, x, 1) + up(other0)
    sum1 = half1[0] + sum(up(part) for part in got1)
    scores, blocks = [], []
    for e, (pre, upw) in enumerate((sum0, sum1)):
        gate = lax.dynamic_slice_in_dim(gates[e], spot * 64, 64, 0)
        value, slope = gelu_pair(pre)
        act = value.astype(bf16)
        pre_grad = (gate * upw * slope).astype(bf16)
        scores.append(jnp.sum(up(act) * upw, axis=1))
        blocks.append(jnp.stack([act, pre_grad]))

    score = jnp.broadcast_to(jnp.stack(scores).reshape(1, 1, -1), (128, 1, 128))
    sent0, sent1, score = together(*blocks, score)
    other0, ring1, score = together(
        send_x(sent0), ring(sent1, send_y), score
    )
    pair0, ring1, score = together(
        join_x(sent0, other0, x, 1).reshape(2, 128, -1), jnp.stack(ring1), score
    )
    *wide, score = together(
        ring(pair0, send_y), [ring1, send_x(ring1)], trade_all(score)
    )
    score = jnp.sum(score.reshape(2, 4, 2, 8, flight, 2, span), axis=0)
    score = jnp.stack(
        [
            score[:, :, :, 0].reshape(4, 2, 2, 4, 2, span),
            score[:, :, :, 1].reshape(4, 2, 2, 2, 4, span).transpose(0, 1, 2, 4, 3, 5),
        ]
    )
    places = jnp.arange(4)
    hit = (places[:, None, None] + places[None, :, None]) % 4 == places[None, None, :]
    score = jnp.sum(
        jnp.where(
            hit.reshape(1, 4, 1, 1, 4, 4, 1, 1), score[:, :, :, :, :, None], jnp.zeros((), f32)
        ),
        axis=(1, 4),
    )
    score = jnp.stack(
        [score[:, 0, 0] + score[:, 1, 1], score[:, 0, 1] + score[:, 1, 0]], axis=1
    ).transpose(0, 1, 3, 2, 4)

    back = []
    for e in range(flight):
        kept, sent = row_terms_of(wide[e], w_in, e, spots)
        back.append(kept + up(send_core(sent)))
    sent = jnp.stack(back, axis=2).astype(bf16).reshape(8, flight, span, feature_width)
    row_grads = jnp.sum(up(trade_places(sent)), axis=0).astype(bf16)
    grads = ()
    for e in range(flight):
        grads = weight_grads(
            near[e], far[e], after(gates[e], sent), wide[e], e, spots, grads
        )
    w_in_grad, w_out_grad = grads

    home = lax.all_to_all(
        after(row_grads, w_in_grad).reshape(flight, 8, capacity, feature_width)
        .transpose(1, 0, 2, 3)
        .reshape(8, flight * capacity, feature_width),
        "local",
        0,
        0,
        tiled=True,
    )
    home = home.transpose(1, 0, 2).reshape(flight * capacity, model_width)

    own_scores = pick(pick(pick(score, core, 1), x_hi, 1), z, 1)
    own_scores = pick(own_scores.reshape(flight, 8, capacity), spot, 1).reshape(-1)
    score = turned(join_x(score[:, 0], score[:, 1], core, 1), turns, 3)
    swapped = score.transpose(0, 1, 3, 2, 4)
    score = [swapped[0], score[1]]

    router_terms = jnp.zeros((), f32)
    for e in range(flight):
        fact = up(facts[e])
        probs = fact[:, :expert_count]
        mine = jnp.arange(expert_count) == e
        grad = jnp.where(mine, score[e].reshape(-1, 1), jnp.zeros((), f32))
        if e == 0:
            twin = fact[:, expert_count : expert_count + capacity]
            twin = twin * jnp.repeat(swapped[1].reshape(-1, capacity), capacity, axis=0)
            twin = jnp.sum(twin, axis=1, keepdims=True)
            grad = jnp.where(jnp.arange(expert_count) == 1, twin, grad)
        else:
            grad = grad * fact[:, expert_count + capacity : expert_count + capacity + 1]
        centred = grad - jnp.sum(probs * grad, axis=1, keepdims=True)
        logits = (probs * centred).astype(bf16)
        columns = jnp.stack([near[e], far[e]])[:, :, :span]
        columns = lax.dynamic_slice_in_dim(columns, node * 64, 64, 3).reshape(-1, 64)
        router_terms = router_terms + contract(columns, logits, 0, 0)
    router_grad = lax.ppermute(
        router_terms, ("node", "local"), [(i, i % 8 * 16 + i // 8) for i in range(128)]
    )

    gate_grad = jnp.sum(
        jnp.where(slot_hits, own_scores[:, None, None], jnp.zeros((), f32)), axis=0
    )
    expert_iota = jnp.arange(expert_count, dtype=jnp.int32)
    matches = expert_ids[:, :, None] == expert_iota[None, None, :]
    prob_grad = jnp.sum(
        jnp.where(matches, gate_grad[:, :, None], jnp.zeros((), f32)), axis=1
    )
    centred = prob_grad - jnp.sum(router_probs * prob_grad, axis=1, keepdims=True)
    logit_grad = (router_probs * centred).astype(bf16)

    combined = contract(placing, home, 0, 0)
    router_part = contract(logit_grad, router_weight, 1, 1)
    token_grads = (combined + router_part).astype(bf16)
    return (token_grads, w_in_grad, w_out_grad, router_grad)


def solution(mesh):
    in_specs = (
        P(("node", "local"), None),
        P(("node", "local"), None),
        P(("node", "local"), None),
        P(("node", "local"), None),
        P(("node", "local"), None),
        P(None, "local", "node"),
        P(None, "node", "local"),
        P(),
    )
    out_specs = (
        P(("node", "local"), None),
        P(None, "local", "node"),
        P(None, "node", "local"),
        P(("node", "local"), None),
    )
    return jax.shard_map(local, mesh=mesh, in_specs=in_specs, out_specs=out_specs, check_vma=False)
```

```python
import math

import jax
import jax.numpy as jnp
from jax import lax
from jax.experimental import pallas as pl
from jax.experimental.pallas import tpu as pltpu
from jax.sharding import PartitionSpec as P

CAP = 4


root_two_pi = math.sqrt(2.0 / math.pi)
cubic_coef = 0.044715
bf16 = jnp.bfloat16
f32 = jnp.float32


def gelu_pair(pre):
    inner = root_two_pi * (pre + cubic_coef * pre * pre * pre)
    tangent = jnp.tanh(inner)
    value = 0.5 * pre * (1.0 + tangent)
    slope = 0.5 * (1.0 + tangent) + 0.5 * pre * (1.0 - tangent * tangent) * root_two_pi * (
        1.0 + 3.0 * cubic_coef * pre * pre
    )
    return (value, slope)


def contract(left, right, left_dim, right_dim):
    return lax.dot_general(
        left, right, (((left_dim,), (right_dim,)), ((), ())), preferred_element_type=f32
    )


same_core = [[place * 2 + core for place in range(8)] for core in range(2)]


def send_core(value):
    return lax.ppermute(value, "node", [(i, i ^ 1) for i in range(16)])


def send_x_hi(value):
    return lax.ppermute(value, "node", [(i, i ^ 8) for i in range(16)])


def send_x(value):
    return lax.ppermute(value, "local", [(i, i ^ 1) for i in range(8)])


def trade_places(blocks):
    return lax.all_to_all(blocks, "node", 0, 0, tiled=True, axis_index_groups=same_core)


def send_z(value, step):
    pairs = [(i, (i // 8 * 4 + (i // 2 + step) % 4) * 2 + i % 2) for i in range(16)]
    return lax.ppermute(value, "node", pairs)


def send_y(value, step):
    return lax.ppermute(value, "local", [(i, (i // 2 + step) % 4 * 2 + i % 2) for i in range(8)])


def ring(value, send):
    return [value] + [send(value, 4 - step) for step in range(1, 4)]


def turn(start):
    places = jnp.arange(4)
    return (places[:, None] + start) % 4 == places[None, :]


def turned(value, hit, axis):
    value = jnp.moveaxis(value, axis, 0)
    hit = hit.reshape((4, 4) + (1,) * (value.ndim - 1))
    return jnp.moveaxis(jnp.sum(jnp.where(hit, value[None], jnp.zeros((), f32)), axis=1), 0, axis)


def trade_all(value):
    return lax.all_to_all(value, ("node", "local"), 0, 0, tiled=True)


def spread(value, count):
    return jnp.broadcast_to(value[None], (count,) + value.shape)


def after(value, *others):
    return lax.optimization_barrier((value,) + others)[0]


def together(*values):
    return lax.optimization_barrier(values)


def up(value):
    return value.astype(f32)


def pick(value, index, axis):
    return lax.dynamic_index_in_dim(value, index, axis, keepdims=False)


def join_x(mine, other, x, axis):
    return jnp.stack([jnp.where(x == 0, mine, other), jnp.where(x == 0, other, mine)], axis=axis)


def matmul(left, right, left_dim=1, right_dim=0):
    return contract(left, right, left_dim, right_dim)


tile = 256
room = 58 * 1024 * 1024


def call(kernel, grid, in_specs, out_specs, out_shape, flops, scratch=(), aliases=None):
    return pl.pallas_call(
        kernel,
        grid=grid,
        in_specs=in_specs,
        out_specs=out_specs,
        out_shape=out_shape,
        scratch_shapes=list(scratch),
        input_output_aliases=aliases or {},
        compiler_params=pltpu.CompilerParams(vmem_limit_bytes=room),
        cost_estimate=pl.CostEstimate(flops=flops, bytes_accessed=flops // 256, transcendentals=0),
    )


def row_specs():
    return [pl.BlockSpec((8, 32, 1024), lambda j, k=k: (0, k, 0)) for k in (0, 1, 0, 1)]


scalar_spec = pl.BlockSpec(memory_space=pltpu.SMEM)


step_width = 256


def weight_specs(e):
    return [
        pl.BlockSpec((1, 1024, step_width), lambda j: (e, 0, j)),
        pl.BlockSpec((1, step_width, 1024), lambda j: (e, j, 0)),
    ]


def projections(refs, rows):
    into, out_of = refs[4:]

    @pl.when(pl.program_id(0) == 0)
    def _():
        for part in range(4):
            half = part // 2 * 256
            rows[part % 2, half : half + 256, :] = refs[part][...].reshape(256, 1024)

    return matmul(rows[0], into[0]), matmul(rows[1], out_of[0], 1, 1)


def project_whole(near, far, w_in, w_out, e, spots):
    def kernel(at, *refs):
        outs, rows, parts = refs[6:10], refs[10], refs[11]
        for which, part in enumerate(projections(refs[:6], rows)):
            parts[:, which] = part.astype(bf16).reshape(4, 128, step_width)
        for step in range(4):
            outs[step][...] = parts[lax.rem(at[0] + step, 4)]

    return call(
        kernel,
        (1024 // step_width,),
        [scalar_spec] + row_specs() + weight_specs(e),
        [pl.BlockSpec((2, 128, step_width), lambda j: (0, 0, j))] * 4,
        [jax.ShapeDtypeStruct((2, 128, 1024), bf16)] * 4,
        2 * 2 * 512 * 1024 * 1024,
        [pltpu.VMEM((2, 512, 1024), bf16), pltpu.VMEM((4, 2, 128, step_width), bf16)],
    )(spots, near, near, far, far, w_in, w_out)


def project_split(near, far, w_in, w_out, e, spots):
    def kernel(at, *refs):
        kept, sent, rows = refs[6:]
        first = at[1] == 0
        for which, part in enumerate(projections(refs[:6], rows)):
            part = part.astype(bf16).reshape(4, 2, 64, step_width)
            low, high = part[:, 0], part[:, 1]
            mine, other = jnp.where(first, low, high), jnp.where(first, high, low)
            for y in range(4):
                place = lax.rem(y + 4 - at[0], 4)
                kept[place, which] = mine[y]
                sent[place, which] = other[y]

    return call(
        kernel,
        (1024 // step_width,),
        [scalar_spec] + row_specs() + weight_specs(e),
        [pl.BlockSpec((4, 2, 64, step_width), lambda j: (0, 0, 0, j))] * 2,
        [jax.ShapeDtypeStruct((4, 2, 64, 1024), bf16)] * 2,
        2 * 2 * 512 * 1024 * 1024,
        [pltpu.VMEM((2, 512, 1024), bf16)],
    )(spots, near, near, far, far, w_in, w_out)


def wide_specs(pieces, which):
    if len(pieces) == 4:
        return [pl.BlockSpec((1, 128, 1024), lambda j: (which, 0, 0))] * 4
    return [pl.BlockSpec((4, 1, 64, 1024), lambda j: (0, which, 0, 0))] * 2


def lay_rows(pieces, at, rows):
    for step in range(4):
        base = lax.rem(at[0] + step, 4) * 128
        if len(pieces) == 4:
            rows[pl.ds(pl.multiple_of(base, 128), 128), :] = pieces[step][0]
        else:
            for x, piece in ((at[1], pieces[0]), (1 - at[1], pieces[1])):
                rows[pl.ds(pl.multiple_of(base + x * 64, 64), 64), :] = piece[step, 0]


def row_terms_of(pieces, w_in, e, spots):
    count = len(pieces)
    wide = 512

    def kernel(at, *refs):
        grads, into, kept, sent, rows = refs[:count], *refs[count:]

        @pl.when(pl.program_id(0) == 0)
        def _():
            lay_rows(grads, at, rows)

        terms = matmul(rows[...], into[0], 1, 1)
        for step in range(4):
            z = lax.rem(at[2] + step, 4)
            for x_hi in range(2):
                block = (step * 2 + x_hi if e == 0 else x_hi * 4 + step) * 32
                kept[x_hi, z] = terms[block : block + 32]
                sent[x_hi, z] = terms[256 + block : 288 + block].astype(bf16)

    shape = (2, 4, 32, 1024)
    return call(
        kernel,
        (1024 // wide,),
        [scalar_spec]
        + wide_specs(pieces, 1)
        + [pl.BlockSpec((1, wide, 1024), lambda j: (e, j, 0))],
        [pl.BlockSpec((2, 4, 32, wide), lambda j: (0, 0, 0, j))] * 2,
        [jax.ShapeDtypeStruct(shape, f32), jax.ShapeDtypeStruct(shape, bf16)],
        2 * 512 * 1024 * 1024,
        [pltpu.VMEM((512, 1024), bf16)],
    )(spots, *pieces, w_in)


def weight_grads(near, far, gates, pieces, e, spots, earlier=()):
    count = len(pieces)

    def kernel(at, in0, up0, in1, up1, gate, *refs):
        acts, grads, refs = refs[:count], refs[count : 2 * count], refs[2 * count + len(earlier) :]
        into, out_of, act_rows, grad_rows, out_rows = refs
        j = pl.program_id(0)

        @pl.when(j == 0)
        def _():
            lay_rows(acts, at, act_rows)
            lay_rows(grads, at, grad_rows)
            for half, ups in enumerate((up0, up1)):
                part = slice(256 * half, 256 * half + 256)
                out_rows[part, :] = (
                    up(ups[...].reshape(256, 1024)) * gate[part, :]
                ).astype(bf16)

        columns = pl.ds(pl.multiple_of(j * tile, tile), tile)
        into[0] = (
            matmul(in0[:, :, columns].reshape(256, tile), grad_rows[:256, :], 0, 0)
            + matmul(in1[:, :, columns].reshape(256, tile), grad_rows[256:, :], 0, 0)
        ).astype(bf16)
        out_of[0] = matmul(act_rows[:, columns], out_rows[...], 0, 0).astype(bf16)

    return call(
        kernel,
        (1024 // tile,),
        [scalar_spec]
        + row_specs()
        + [pl.BlockSpec((512, 1), lambda j: (0, 0))]
        + wide_specs(pieces, 0)
        + wide_specs(pieces, 1)
        + [pl.BlockSpec(memory_space=pl.ANY)] * len(earlier),
        [pl.BlockSpec((1, tile, 1024), lambda j: (e, j, 0))] * 2,
        [jax.ShapeDtypeStruct((2, 1024, 1024), bf16)] * 2,
        2 * 2 * 512 * 1024 * 1024,
        [pltpu.VMEM((512, 1024), bf16)] * 3,
        {6 + 2 * count + i: i for i in range(len(earlier))},
    )(spots, near, near, far, far, gates, *pieces, *pieces, *earlier)


def local(tokens, upstream, router_probs, expert_ids, slot_index, w_in, w_out, router_weight):
    token_count, model_width = tokens.shape
    flight = w_in.shape[0]
    feature_width = w_in.shape[1]
    capacity = CAP
    expert_count = router_probs.shape[1]
    node = lax.axis_index("node")
    spot = lax.axis_index("local")
    x_hi, z, core, y, x = node // 8, node // 2 % 4, node % 2, spot // 2, spot % 2
    spots = jnp.stack([y, x, z]).astype(jnp.int32)
    span = 8 * capacity

    is_kept = slot_index >= 0
    target = jnp.where(is_kept, expert_ids * capacity + slot_index, -1)
    slot_iota = jnp.arange(flight * capacity, dtype=jnp.int32)
    slot_hits = slot_iota[:, None, None] == target[None, :, :]
    placing = jnp.any(slot_hits, axis=2).astype(bf16)
    send_in = jnp.dot(placing, tokens, preferred_element_type=f32).astype(bf16)
    send_up = jnp.dot(placing, upstream, preferred_element_type=f32).astype(bf16)
    slot_probs = jnp.dot(placing, router_probs.astype(bf16), preferred_element_type=f32)
    same = contract(placing, placing, 1, 1)
    twins = same[:, 4:]
    counted = 1 - jnp.where(slot_iota < 4, 0, jnp.sum(same[:, :4], axis=1))[:, None]
    facts = jnp.pad(
        jnp.concatenate([slot_probs, twins, counted], axis=1).astype(bf16), ((0, 8), (0, 59))
    )
    blocks = jnp.stack([send_in, send_up]).reshape(16, 8, feature_width).transpose(1, 0, 2)
    got = lax.all_to_all(
        jnp.concatenate([blocks, spread(facts, 8)], axis=2), "local", 0, 0, tiled=True
    )
    facts = (
        got[:, :8, feature_width:].reshape(8, flight, capacity, 128)
        .transpose(1, 0, 2, 3)
        .reshape(8, 8, 128)
        .transpose(1, 0, 2)
        .reshape(8, feature_width)
    )
    got = (
        got[:, :, :feature_width]
        .reshape(8, 2, flight, capacity, feature_width)
        .transpose(2, 1, 0, 3, 4)
        .reshape(4 * span, feature_width)
    )
    packets = [got[: 2 * span], jnp.concatenate([got[2 * span :], facts])]

    pair0 = join_x(packets[0], send_x_hi(packets[0]), x_hi, 0)
    ring1 = jnp.stack(ring(packets[1], send_z))
    pair0, ring1 = together(pair0, ring1)
    near1 = join_x(ring1, send_x_hi(ring1), x_hi, 0).reshape(8, -1, feature_width)
    near0 = jnp.stack(ring(pair0, send_z)).reshape(8, -1, feature_width)
    near0, near1, turns = together(near0, near1, turn(z))
    near, far = [near0, near1], [send_core(near0), send_core(near1)]
    facts = (
        jnp.stack([near1[:, 2 * span :], far[1][:, 2 * span :]])
        .reshape(16, 8, 8, 128)
        .transpose(0, 2, 1, 3)
        .reshape(16, flight, span, 128)
    )
    facts = [
        facts[:, 0].reshape(2, 2, 4, span, 128).transpose(0, 2, 1, 3, 4).reshape(-1, 128),
        facts[:, 1].reshape(-1, 128),
    ]
    gates = [up(facts[e][:, e : e + 1]) for e in range(flight)]

    kept1, sent1 = project_split(near[1], far[1], w_in, w_out, 1, spots)
    other1 = send_x(sent1)
    parts0 = project_whole(after(near[0], sent1), far[0], w_in, w_out, 0, spots)
    got0 = [send_y(parts0[step], step) for step in (2, 1, 3)]
    other1, got0 = together(other1, got0)
    half0 = (up(parts0[0]) + sum(up(part) for part in got0)).reshape(2, 2, 64, -1)
    half1 = [up(kept1[step]) + up(other1[step]) for step in range(4)]
    sent0, sent1 = together(
        pick(half0, 1 - x, 1).astype(bf16), [half1[step].astype(bf16) for step in range(1, 4)]
    )
    other0, got1 = together(
        send_x(sent0), [send_y(part, step + 1) for step, part in enumerate(sent1)]
    )
    sum0 = pick(half0, x, 1) + up(other0)
    sum1 = half1[0] + sum(up(part) for part in got1)
    scores, blocks = [], []
    for e, (pre, upw) in enumerate((sum0, sum1)):
        gate = lax.dynamic_slice_in_dim(gates[e], spot * 64, 64, 0)
        value, slope = gelu_pair(pre)
        act = value.astype(bf16)
        pre_grad = (gate * upw * slope).astype(bf16)
        scores.append(jnp.sum(up(act) * upw, axis=1))
        blocks.append(jnp.stack([act, pre_grad]))

    score = jnp.broadcast_to(jnp.stack(scores).reshape(1, 1, -1), (128, 1, 128))
    sent0, sent1, score = together(*blocks, score)
    other0, ring1, score = together(
        send_x(sent0), ring(sent1, send_y), score
    )
    pair0, ring1, score = together(
        join_x(sent0, other0, x, 1).reshape(2, 128, -1), ring1, score
    )
    ring1 = jnp.stack(ring1)
    *wide, score = together(
        ring(pair0, send_y), [ring1, send_x(ring1)], trade_all(score)
    )
    back = []
    for e in range(flight):
        kept, sent = row_terms_of(wide[e], w_in, e, spots)
        back.append(kept + up(send_core(sent)))
    sent = jnp.stack(back, axis=2).astype(bf16).reshape(8, flight, span, feature_width)

    score = jnp.sum(after(score, sent).reshape(2, 4, 2, 8, flight, 2, span), axis=0)
    score = jnp.stack(
        [
            score[:, :, :, 0].reshape(4, 2, 2, 4, 2, span),
            score[:, :, :, 1].reshape(4, 2, 2, 2, 4, span).transpose(0, 1, 2, 4, 3, 5),
        ]
    )
    places = jnp.arange(4)
    hit = (places[:, None, None] + places[None, :, None]) % 4 == places[None, None, :]
    score = jnp.sum(
        jnp.where(
            hit.reshape(1, 4, 1, 1, 4, 4, 1, 1), score[:, :, :, :, :, None], jnp.zeros((), f32)
        ),
        axis=(1, 4),
    )
    score = jnp.stack(
        [score[:, 0, 0] + score[:, 1, 1], score[:, 0, 1] + score[:, 1, 0]], axis=1
    ).transpose(0, 1, 3, 2, 4)

    row_grads = jnp.sum(up(trade_places(sent)), axis=0).astype(bf16)
    grads = weight_grads(near[0], far[0], after(gates[0], sent), wide[0], 0, spots)
    row_grads = after(row_grads, grads[0])
    grads = weight_grads(near[1], far[1], after(gates[1], row_grads), wide[1], 1, spots, grads)
    w_in_grad, w_out_grad = grads

    home = lax.all_to_all(
        row_grads.reshape(flight, 8, capacity, feature_width)
        .transpose(1, 0, 2, 3)
        .reshape(8, flight * capacity, feature_width),
        "local",
        0,
        0,
        tiled=True,
    )
    home = home.transpose(1, 0, 2).reshape(flight * capacity, model_width)

    own_scores = pick(pick(pick(score, core, 1), x_hi, 1), z, 1)
    own_scores = pick(own_scores.reshape(flight, 8, capacity), spot, 1).reshape(-1)
    score = turned(join_x(score[:, 0], score[:, 1], core, 1), turns, 3)
    swapped = score.transpose(0, 1, 3, 2, 4)
    score = [swapped[0], score[1]]

    router_terms = jnp.zeros((), f32)
    for e in range(flight):
        fact = up(facts[e])
        probs = fact[:, :expert_count]
        mine = jnp.arange(expert_count) == e
        grad = jnp.where(mine, score[e].reshape(-1, 1), jnp.zeros((), f32))
        if e == 0:
            twin = fact[:, expert_count : expert_count + capacity]
            twin = twin * jnp.repeat(swapped[1].reshape(-1, capacity), capacity, axis=0)
            twin = jnp.sum(twin, axis=1, keepdims=True)
            grad = jnp.where(jnp.arange(expert_count) == 1, twin, grad)
        else:
            grad = grad * fact[:, expert_count + capacity : expert_count + capacity + 1]
        centred = grad - jnp.sum(probs * grad, axis=1, keepdims=True)
        logits = (probs * centred).astype(bf16)
        columns = jnp.stack([near[e], far[e]])[:, :, :span]
        columns = lax.dynamic_slice_in_dim(columns, node * 64, 64, 3).reshape(-1, 64)
        router_terms = router_terms + contract(columns, logits, 0, 0)
    router_grad = lax.ppermute(
        router_terms, ("node", "local"), [(i, i % 8 * 16 + i // 8) for i in range(128)]
    )

    gate_grad = jnp.sum(
        jnp.where(slot_hits, own_scores[:, None, None], jnp.zeros((), f32)), axis=0
    )
    expert_iota = jnp.arange(expert_count, dtype=jnp.int32)
    matches = expert_ids[:, :, None] == expert_iota[None, None, :]
    prob_grad = jnp.sum(
        jnp.where(matches, gate_grad[:, :, None], jnp.zeros((), f32)), axis=1
    )
    centred = prob_grad - jnp.sum(router_probs * prob_grad, axis=1, keepdims=True)
    logit_grad = (router_probs * centred).astype(bf16)

    combined = contract(placing, home, 0, 0)
    router_part = contract(logit_grad, router_weight, 1, 1)
    token_grads = (combined + router_part).astype(bf16)
    return (token_grads, w_in_grad, w_out_grad, router_grad)


def solution(mesh):
    in_specs = (
        P(("node", "local"), None),
        P(("node", "local"), None),
        P(("node", "local"), None),
        P(("node", "local"), None),
        P(("node", "local"), None),
        P(None, "local", "node"),
        P(None, "node", "local"),
        P(),
    )
    out_specs = (
        P(("node", "local"), None),
        P(None, "local", "node"),
        P(None, "node", "local"),
        P(("node", "local"), None),
    )
    return jax.shard_map(local, mesh=mesh, in_specs=in_specs, out_specs=out_specs, check_vma=False)
```

```python
import math

import jax
import jax.numpy as jnp
from jax import lax
from jax.experimental import pallas as pl
from jax.experimental.pallas import tpu as pltpu
from jax.sharding import PartitionSpec as P

CAP = 4


root_two_pi = math.sqrt(2.0 / math.pi)
cubic_coef = 0.044715
bf16 = jnp.bfloat16
f32 = jnp.float32


def gelu_pair(pre):
    inner = root_two_pi * (pre + cubic_coef * pre * pre * pre)
    tangent = jnp.tanh(inner)
    value = 0.5 * pre * (1.0 + tangent)
    slope = 0.5 * (1.0 + tangent) + 0.5 * pre * (1.0 - tangent * tangent) * root_two_pi * (
        1.0 + 3.0 * cubic_coef * pre * pre
    )
    return (value, slope)


def contract(left, right, left_dim, right_dim):
    return lax.dot_general(
        left, right, (((left_dim,), (right_dim,)), ((), ())), preferred_element_type=f32
    )


same_core = [[place * 2 + core for place in range(8)] for core in range(2)]


def send_core(value):
    return lax.ppermute(value, "node", [(i, i ^ 1) for i in range(16)])


def send_x_hi(value):
    return lax.ppermute(value, "node", [(i, i ^ 8) for i in range(16)])


def send_x(value):
    return lax.ppermute(value, "local", [(i, i ^ 1) for i in range(8)])


def trade_places(blocks):
    return lax.all_to_all(blocks, "node", 0, 0, tiled=True, axis_index_groups=same_core)


def send_z(value, step):
    pairs = [(i, (i // 8 * 4 + (i // 2 + step) % 4) * 2 + i % 2) for i in range(16)]
    return lax.ppermute(value, "node", pairs)


def send_y(value, step):
    return lax.ppermute(value, "local", [(i, (i // 2 + step) % 4 * 2 + i % 2) for i in range(8)])


def ring(value, send):
    return [value] + [send(value, 4 - step) for step in range(1, 4)]


def turn(start):
    places = jnp.arange(4)
    return (places[:, None] + start) % 4 == places[None, :]


def turned(value, hit, axis):
    value = jnp.moveaxis(value, axis, 0)
    hit = hit.reshape((4, 4) + (1,) * (value.ndim - 1))
    return jnp.moveaxis(jnp.sum(jnp.where(hit, value[None], jnp.zeros((), f32)), axis=1), 0, axis)


def trade_all(value):
    return lax.all_to_all(value, ("node", "local"), 0, 0, tiled=True)


def spread(value, count):
    return jnp.broadcast_to(value[None], (count,) + value.shape)


def after(value, *others):
    return lax.optimization_barrier((value,) + others)[0]


def together(*values):
    return lax.optimization_barrier(values)


def up(value):
    return value.astype(f32)


def pick(value, index, axis):
    return lax.dynamic_index_in_dim(value, index, axis, keepdims=False)


def join_x(mine, other, x, axis):
    return jnp.stack([jnp.where(x == 0, mine, other), jnp.where(x == 0, other, mine)], axis=axis)


def matmul(left, right, left_dim=1, right_dim=0):
    return contract(left, right, left_dim, right_dim)


tile = 256
room = 58 * 1024 * 1024


def call(kernel, grid, in_specs, out_specs, out_shape, flops, scratch=(), aliases=None):
    return pl.pallas_call(
        kernel,
        grid=grid,
        in_specs=in_specs,
        out_specs=out_specs,
        out_shape=out_shape,
        scratch_shapes=list(scratch),
        input_output_aliases=aliases or {},
        compiler_params=pltpu.CompilerParams(vmem_limit_bytes=room),
        cost_estimate=pl.CostEstimate(flops=flops, bytes_accessed=flops // 256, transcendentals=0),
    )


def row_specs():
    return [pl.BlockSpec((8, 32, 1024), lambda j, k=k: (0, k, 0)) for k in (0, 1, 0, 1)]


scalar_spec = pl.BlockSpec(memory_space=pltpu.SMEM)


step_width = 256


def weight_specs(e):
    return [
        pl.BlockSpec((1, 1024, step_width), lambda j: (e, 0, j)),
        pl.BlockSpec((1, step_width, 1024), lambda j: (e, j, 0)),
    ]


def projections(refs, rows):
    into, out_of = refs[4:]

    @pl.when(pl.program_id(0) == 0)
    def _():
        for part in range(4):
            half = part // 2 * 256
            rows[part % 2, half : half + 256, :] = refs[part][...].reshape(256, 1024)

    return matmul(rows[0], into[0]), matmul(rows[1], out_of[0], 1, 1)


def project_whole(near, far, w_in, w_out, e, spots):
    def kernel(at, *refs):
        outs, rows, parts = refs[6:10], refs[10], refs[11]
        for which, part in enumerate(projections(refs[:6], rows)):
            parts[:, which] = part.astype(bf16).reshape(4, 128, step_width)
        for step in range(4):
            outs[step][...] = parts[lax.rem(at[0] + step, 4)]

    return call(
        kernel,
        (1024 // step_width,),
        [scalar_spec] + row_specs() + weight_specs(e),
        [pl.BlockSpec((2, 128, step_width), lambda j: (0, 0, j))] * 4,
        [jax.ShapeDtypeStruct((2, 128, 1024), bf16)] * 4,
        2 * 2 * 512 * 1024 * 1024,
        [pltpu.VMEM((2, 512, 1024), bf16), pltpu.VMEM((4, 2, 128, step_width), bf16)],
    )(spots, near, near, far, far, w_in, w_out)


def project_split(near, far, w_in, w_out, e, spots):
    def kernel(at, *refs):
        kept, sent, rows = refs[6:]
        first = at[1] == 0
        for which, part in enumerate(projections(refs[:6], rows)):
            part = part.astype(bf16).reshape(4, 2, 64, step_width)
            low, high = part[:, 0], part[:, 1]
            mine, other = jnp.where(first, low, high), jnp.where(first, high, low)
            for y in range(4):
                place = lax.rem(y + 4 - at[0], 4)
                kept[place, which] = mine[y]
                sent[place, which] = other[y]

    return call(
        kernel,
        (1024 // step_width,),
        [scalar_spec] + row_specs() + weight_specs(e),
        [pl.BlockSpec((4, 2, 64, step_width), lambda j: (0, 0, 0, j))] * 2,
        [jax.ShapeDtypeStruct((4, 2, 64, 1024), bf16)] * 2,
        2 * 2 * 512 * 1024 * 1024,
        [pltpu.VMEM((2, 512, 1024), bf16)],
    )(spots, near, near, far, far, w_in, w_out)


def wide_specs(pieces, which):
    if len(pieces) == 4:
        return [pl.BlockSpec((1, 128, 1024), lambda j: (which, 0, 0))] * 4
    return [pl.BlockSpec((4, 1, 64, 1024), lambda j: (0, which, 0, 0))] * 2


def lay_rows(pieces, at, rows):
    for step in range(4):
        base = lax.rem(at[0] + step, 4) * 128
        if len(pieces) == 4:
            rows[pl.ds(pl.multiple_of(base, 128), 128), :] = pieces[step][0]
        else:
            for x, piece in ((at[1], pieces[0]), (1 - at[1], pieces[1])):
                rows[pl.ds(pl.multiple_of(base + x * 64, 64), 64), :] = piece[step, 0]


def row_terms_of(pieces, w_in, e, spots):
    count = len(pieces)
    wide = 512

    def kernel(at, *refs):
        grads, into, kept, sent, rows = refs[:count], *refs[count:]

        @pl.when(pl.program_id(0) == 0)
        def _():
            lay_rows(grads, at, rows)

        terms = matmul(rows[...], into[0], 1, 1)
        for step in range(4):
            z = lax.rem(at[2] + step, 4)
            for x_hi in range(2):
                block = (step * 2 + x_hi if e == 0 else x_hi * 4 + step) * 32
                kept[x_hi, z] = terms[block : block + 32]
                sent[x_hi, z] = terms[256 + block : 288 + block].astype(bf16)

    shape = (2, 4, 32, 1024)
    return call(
        kernel,
        (1024 // wide,),
        [scalar_spec]
        + wide_specs(pieces, 1)
        + [pl.BlockSpec((1, wide, 1024), lambda j: (e, j, 0))],
        [pl.BlockSpec((2, 4, 32, wide), lambda j: (0, 0, 0, j))] * 2,
        [jax.ShapeDtypeStruct(shape, f32), jax.ShapeDtypeStruct(shape, bf16)],
        2 * 512 * 1024 * 1024,
        [pltpu.VMEM((512, 1024), bf16)],
    )(spots, *pieces, w_in)


def weight_grads(near, far, gates, pieces, e, spots, earlier=()):
    count = len(pieces)

    def kernel(at, in0, up0, in1, up1, gate, *refs):
        acts, grads, refs = refs[:count], refs[count : 2 * count], refs[2 * count + len(earlier) :]
        into, out_of, act_rows, grad_rows, out_rows = refs
        j = pl.program_id(0)

        @pl.when(j == 0)
        def _():
            lay_rows(acts, at, act_rows)
            lay_rows(grads, at, grad_rows)
            for half, ups in enumerate((up0, up1)):
                part = slice(256 * half, 256 * half + 256)
                out_rows[part, :] = (
                    up(ups[...].reshape(256, 1024)) * gate[part, :]
                ).astype(bf16)

        columns = pl.ds(pl.multiple_of(j * tile, tile), tile)
        into[0] = (
            matmul(in0[:, :, columns].reshape(256, tile), grad_rows[:256, :], 0, 0)
            + matmul(in1[:, :, columns].reshape(256, tile), grad_rows[256:, :], 0, 0)
        ).astype(bf16)
        out_of[0] = matmul(act_rows[:, columns], out_rows[...], 0, 0).astype(bf16)

    return call(
        kernel,
        (1024 // tile,),
        [scalar_spec]
        + row_specs()
        + [pl.BlockSpec((512, 1), lambda j: (0, 0))]
        + wide_specs(pieces, 0)
        + wide_specs(pieces, 1)
        + [pl.BlockSpec(memory_space=pl.ANY)] * len(earlier),
        [pl.BlockSpec((1, tile, 1024), lambda j: (e, j, 0))] * 2,
        [jax.ShapeDtypeStruct((2, 1024, 1024), bf16)] * 2,
        2 * 2 * 512 * 1024 * 1024,
        [pltpu.VMEM((512, 1024), bf16)] * 3,
        {6 + 2 * count + i: i for i in range(len(earlier))},
    )(spots, near, near, far, far, gates, *pieces, *pieces, *earlier)


def local(tokens, upstream, router_probs, expert_ids, slot_index, w_in, w_out, router_weight):
    token_count, model_width = tokens.shape
    flight = w_in.shape[0]
    feature_width = w_in.shape[1]
    capacity = CAP
    expert_count = router_probs.shape[1]
    node = lax.axis_index("node")
    spot = lax.axis_index("local")
    x_hi, z, core, y, x = node // 8, node // 2 % 4, node % 2, spot // 2, spot % 2
    spots = jnp.stack([y, x, z]).astype(jnp.int32)
    span = 8 * capacity

    is_kept = slot_index >= 0
    target = jnp.where(is_kept, expert_ids * capacity + slot_index, -1)
    slot_iota = jnp.arange(flight * capacity, dtype=jnp.int32)
    slot_hits = slot_iota[:, None, None] == target[None, :, :]
    placing = jnp.any(slot_hits, axis=2).astype(bf16)
    send_in = jnp.dot(placing, tokens, preferred_element_type=f32).astype(bf16)
    send_up = jnp.dot(placing, upstream, preferred_element_type=f32).astype(bf16)
    slot_probs = jnp.dot(placing, router_probs.astype(bf16), preferred_element_type=f32)
    same = contract(placing, placing, 1, 1)
    twins = same[:, 4:]
    counted = 1 - jnp.where(slot_iota < 4, 0, jnp.sum(same[:, :4], axis=1))[:, None]
    facts = jnp.pad(
        jnp.concatenate([slot_probs, twins, counted], axis=1).astype(bf16), ((0, 8), (0, 59))
    )
    blocks = jnp.stack([send_in, send_up]).reshape(16, 8, feature_width).transpose(1, 0, 2)
    got = lax.all_to_all(
        jnp.concatenate([blocks, spread(facts, 8)], axis=2), "local", 0, 0, tiled=True
    )
    facts = (
        got[:, :8, feature_width:].reshape(8, flight, capacity, 128)
        .transpose(1, 0, 2, 3)
        .reshape(8, 8, 128)
        .transpose(1, 0, 2)
        .reshape(8, feature_width)
    )
    got = (
        got[:, :, :feature_width]
        .reshape(8, 2, flight, capacity, feature_width)
        .transpose(2, 1, 0, 3, 4)
        .reshape(4 * span, feature_width)
    )
    packets = [got[: 2 * span], jnp.concatenate([got[2 * span :], facts])]

    pair0 = join_x(packets[0], send_x_hi(packets[0]), x_hi, 0)
    ring1 = jnp.stack(ring(packets[1], send_z))
    pair0, ring1 = together(pair0, ring1)
    near1 = join_x(ring1, send_x_hi(ring1), x_hi, 0).reshape(8, -1, feature_width)
    near0 = jnp.stack(ring(pair0, send_z)).reshape(8, -1, feature_width)
    near0, near1, turns = together(near0, near1, turn(z))
    near, far = [near0, near1], [send_core(near0), send_core(near1)]
    facts = (
        jnp.stack([near1[:, 2 * span :], far[1][:, 2 * span :]])
        .reshape(16, 8, 8, 128)
        .transpose(0, 2, 1, 3)
        .reshape(16, flight, span, 128)
    )
    facts = [
        facts[:, 0].reshape(2, 2, 4, span, 128).transpose(0, 2, 1, 3, 4).reshape(-1, 128),
        facts[:, 1].reshape(-1, 128),
    ]
    gates = [up(facts[e][:, e : e + 1]) for e in range(flight)]

    kept1, sent1 = project_split(near[1], far[1], w_in, w_out, 1, spots)
    other1 = send_x(sent1)
    parts0 = project_whole(after(near[0], sent1), far[0], w_in, w_out, 0, spots)
    got0 = [send_y(parts0[step], step) for step in range(1, 4)]
    other1, got0 = together(other1, got0)
    half0 = (up(parts0[0]) + sum(up(part) for part in got0)).reshape(2, 2, 64, -1)
    half1 = [up(kept1[step]) + up(other1[step]) for step in range(4)]
    sent0, sent1 = together(
        pick(half0, 1 - x, 1).astype(bf16), [half1[step].astype(bf16) for step in range(1, 4)]
    )
    other0, got1 = together(
        send_x(sent0), [send_y(part, step + 1) for step, part in enumerate(sent1)]
    )
    sum0 = pick(half0, x, 1) + up(other0)
    sum1 = half1[0] + sum(up(part) for part in got1)
    scores, blocks = [], []
    for e, (pre, upw) in enumerate((sum0, sum1)):
        gate = lax.dynamic_slice_in_dim(gates[e], spot * 64, 64, 0)
        value, slope = gelu_pair(pre)
        act = value.astype(bf16)
        pre_grad = (gate * upw * slope).astype(bf16)
        scores.append(jnp.sum(up(act) * upw, axis=1))
        blocks.append(jnp.stack([act, pre_grad]))

    score = jnp.broadcast_to(jnp.stack(scores).reshape(1, 1, -1), (128, 1, 128))
    sent0, sent1, score = together(*blocks, score)
    other0, ring1, score = together(
        send_x(sent0), ring(sent1, send_y), score
    )
    pair0, ring1, score = together(
        join_x(sent0, other0, x, 1).reshape(2, 128, -1), jnp.stack(ring1), score
    )
    *wide, score = together(
        ring(pair0, send_y), [ring1, send_x(ring1)], trade_all(score)
    )
    score = jnp.sum(score.reshape(2, 4, 2, 8, flight, 2, span), axis=0)
    score = jnp.stack(
        [
            score[:, :, :, 0].reshape(4, 2, 2, 4, 2, span),
            score[:, :, :, 1].reshape(4, 2, 2, 2, 4, span).transpose(0, 1, 2, 4, 3, 5),
        ]
    )
    places = jnp.arange(4)
    hit = (places[:, None, None] + places[None, :, None]) % 4 == places[None, None, :]
    score = jnp.sum(
        jnp.where(
            hit.reshape(1, 4, 1, 1, 4, 4, 1, 1), score[:, :, :, :, :, None], jnp.zeros((), f32)
        ),
        axis=(1, 4),
    )
    score = jnp.stack(
        [score[:, 0, 0] + score[:, 1, 1], score[:, 0, 1] + score[:, 1, 0]], axis=1
    ).transpose(0, 1, 3, 2, 4)

    back = []
    for e in range(flight):
        kept, sent = row_terms_of(wide[e], w_in, e, spots)
        back.append(kept + up(send_core(sent)))
    sent = jnp.stack(back, axis=2).astype(bf16).reshape(8, flight, span, feature_width)
    row_grads = jnp.sum(up(trade_places(sent)), axis=0).astype(bf16)
    grads = ()
    for e in range(flight):
        grads = weight_grads(
            near[e], far[e], after(gates[e], sent), wide[e], e, spots, grads
        )
    w_in_grad, w_out_grad = grads

    home = lax.all_to_all(
        after(row_grads, w_in_grad).reshape(flight, 8, capacity, feature_width)
        .transpose(1, 0, 2, 3)
        .reshape(8, flight * capacity, feature_width),
        "local",
        0,
        0,
        tiled=True,
    )
    home = home.transpose(1, 0, 2).reshape(flight * capacity, model_width)

    own_scores = pick(pick(pick(score, core, 1), x_hi, 1), z, 1)
    own_scores = pick(own_scores.reshape(flight, 8, capacity), spot, 1).reshape(-1)
    score = turned(join_x(score[:, 0], score[:, 1], core, 1), turns, 3)
    swapped = score.transpose(0, 1, 3, 2, 4)
    score = [swapped[0], score[1]]

    router_terms = jnp.zeros((), f32)
    for e in range(flight):
        fact = up(facts[e])
        probs = fact[:, :expert_count]
        mine = jnp.arange(expert_count) == e
        grad = jnp.where(mine, score[e].reshape(-1, 1), jnp.zeros((), f32))
        if e == 0:
            twin = fact[:, expert_count : expert_count + capacity]
            twin = twin * jnp.repeat(swapped[1].reshape(-1, capacity), capacity, axis=0)
            twin = jnp.sum(twin, axis=1, keepdims=True)
            grad = jnp.where(jnp.arange(expert_count) == 1, twin, grad)
        else:
            grad = grad * fact[:, expert_count + capacity : expert_count + capacity + 1]
        centred = grad - jnp.sum(probs * grad, axis=1, keepdims=True)
        logits = (probs * centred).astype(bf16)
        columns = jnp.stack([near[e], far[e]])[:, :, :span]
        columns = lax.dynamic_slice_in_dim(columns, node * 64, 64, 3).reshape(-1, 64)
        router_terms = router_terms + contract(columns, logits, 0, 0)
    router_grad = lax.ppermute(
        router_terms, ("node", "local"), [(i, i % 8 * 16 + i // 8) for i in range(128)]
    )

    gate_grad = jnp.sum(
        jnp.where(slot_hits, own_scores[:, None, None], jnp.zeros((), f32)), axis=0
    )
    expert_iota = jnp.arange(expert_count, dtype=jnp.int32)
    matches = expert_ids[:, :, None] == expert_iota[None, None, :]
    prob_grad = jnp.sum(
        jnp.where(matches, gate_grad[:, :, None], jnp.zeros((), f32)), axis=1
    )
    centred = prob_grad - jnp.sum(router_probs * prob_grad, axis=1, keepdims=True)
    logit_grad = (router_probs * centred).astype(bf16)

    combined = contract(placing, home, 0, 0)
    router_part = lax.optimization_barrier(contract(logit_grad, router_weight, 1, 1))
    token_grads = (combined + router_part).astype(bf16)
    return (token_grads, w_in_grad, w_out_grad, router_grad)


def solution(mesh):
    in_specs = (
        P(("node", "local"), None),
        P(("node", "local"), None),
        P(("node", "local"), None),
        P(("node", "local"), None),
        P(("node", "local"), None),
        P(None, "local", "node"),
        P(None, "node", "local"),
        P(),
    )
    out_specs = (
        P(("node", "local"), None),
        P(None, "local", "node"),
        P(None, "node", "local"),
        P(("node", "local"), None),
    )
    return jax.shard_map(local, mesh=mesh, in_specs=in_specs, out_specs=out_specs, check_vma=False)
```
